32 devices in a mesh: var: 8 (over z, core), blk: 4 (over y, x).
Axes of the slice: x: 2, y: 2, z: 4, core: 2. Of those that a mesh axis runs over, the one named last changes fastest.
Arguments:
- embeddings: float32 [8, 512, 128], P('var', 'blk'), may hold values from -19 to 19, as said below
- spreads: float32 [5], replicated, may hold values from 0.5 to 8
Outputs:
- mmd: float32 [8], P('var')
- gradient: float32 [8, 512, 128], P('var', 'blk')
The draws below stay inside these ranges and needn't reach their ends.
Inputs may be any that keep to these rules, and one draw needn't show every extreme that they name: `embeddings`: each group has its own scale and mean offset, and each event its own scale.
All inputs are finite; a program needn't handle non-finite values.
Results may differ from the reference program's by a relative error of at most 0.00016.
Values sent between devices are 32-bit elements; how exact they have to be, the bound alone decides.
A program may use at most 64 MiB of HBM per device.

```python
import math
import jax
import jax.numpy as jnp
from jax import lax

D = 128
BANDS = 5
EVENTS = 512
VARS = 8


def draw_embeddings(key, part):
    subkeys = jax.random.split(key, 4)
    base = jnp.clip(jax.random.normal(subkeys[0], (VARS, EVENTS, D), jnp.float32), -6.0, 6.0)
    row_scale = jax.random.uniform(subkeys[1], (VARS, EVENTS, 1), jnp.float32, 0.6, 1.4)
    group_scale = jnp.exp(jax.random.uniform(subkeys[2], (VARS, 1, 1), jnp.float32, math.log(0.5), math.log(2.0)))
    offset = jnp.clip(0.5 * jax.random.normal(subkeys[3], (VARS, 1, D), jnp.float32), -2.0, 2.0)
    return (group_scale * row_scale * base + offset).astype(jnp.float32)


def setup_inputs(seed: int = 0) -> dict:
    splits = jax.random.split(jax.random.key(seed), 3)
    return {
        "embeddings": draw_embeddings(jax.random.fold_in(splits[2], 71), 0),
        "spreads": jnp.clip(jnp.exp(jax.random.uniform(splits[1], (BANDS,), jnp.float32, math.log(0.5), math.log(8.0))), 0.5, 8.0),
    }


HIGHEST_PRECISION = lax.Precision.HIGHEST


def kernel_tile(left_rows, right_rows, gains):
    left_sq = jnp.sum(left_rows * left_rows, axis=1)
    right_sq = jnp.sum(right_rows * right_rows, axis=1)
    inner = lax.dot_general(left_rows, right_rows, (((1,), (1,)), ((), ())), precision=HIGHEST_PRECISION, preferred_element_type=jnp.float32)
    distance = left_sq[:, None] + right_sq[None, :] - 2.0 * inner
    kernel_total = jnp.zeros_like(distance)
    weights = jnp.zeros_like(distance)
    band_count = gains.shape[0]
    for band_index in range(band_count):
        decayed = jnp.exp(-distance * gains[band_index])
        kernel_total = kernel_total + decayed
        weights = weights + gains[band_index] * decayed
    return jnp.sum(kernel_total) / band_count, weights / band_count


def matmul_high(left_rows, right_rows):
    return jnp.dot(left_rows, right_rows, precision=HIGHEST_PRECISION, preferred_element_type=jnp.float32)


def reference(embeddings, spreads):
    gains = 1.0 / (D * spreads)
    nominal = embeddings[0]

    def per_group(members):
        self_sum, self_w = kernel_tile(members, members, gains)
        self_grad = -4.0 * (jnp.sum(self_w, axis=1)[:, None] * members - matmul_high(self_w, members))
        cross_sum, cross_w = kernel_tile(nominal, members, gains)
        nominal_part = -2.0 * (jnp.sum(cross_w, axis=1)[:, None] * nominal - matmul_high(cross_w, members))
        member_part = -2.0 * (jnp.sum(cross_w, axis=0)[:, None] * members - matmul_high(cross_w.T, nominal))
        return self_sum, cross_sum, self_grad, nominal_part, member_part

    self_sums, cross_sums, self_grads, nominal_parts, member_parts = lax.map(per_group, embeddings)
    mmd = (self_sums + self_sums[0] - 2.0 * cross_sums) / (EVENTS * EVENTS)
    scale = D / EVENTS
    varied = scale * (self_grads - 2.0 * member_parts)
    nominal_grad = scale * ((VARS - 1) * self_grads[0] - 2.0 * jnp.sum(nominal_parts[1:], axis=0))
    gradient = varied.at[0].set(nominal_grad)
    return mmd, gradient
```

```python
import functools

import jax
import jax.numpy as jnp
from jax import lax
from jax.experimental import pallas as pl
from jax.experimental.pallas import tpu as pltpu
from jax.sharding import PartitionSpec as P

HIGHEST = lax.Precision.HIGHEST
LOG2E = 1.4426950408889634


def partner(index, step, count):
    result = 0
    bit = 1
    while bit < count:
        result = result + ((index // bit + step // bit) % 2) * bit
        bit *= 2
    return result


def dot_t(left, right):
    return lax.dot_general(
        left, right, (((1,), (1,)), ((), ())), precision=HIGHEST, preferred_element_type=jnp.float32
    )


def dot_n(left, right):
    return lax.dot_general(
        left, right, (((1,), (0,)), ((), ())), precision=HIGHEST, preferred_element_type=jnp.float32
    )


def fold(tile):
    return jnp.sum(tile.reshape(tile.shape[0] // 8, 8, tile.shape[1]), axis=0)


def row_square(rows):
    return jnp.sum(rows * rows, axis=1, keepdims=True)


def col_square(rows):
    return dot_t(jnp.ones((8, rows.shape[1]), jnp.float32), rows * rows)[0:1]


def kernel(
    groups, blocks, bands,
    spread_ref, emb_ref, mmd_ref, grad_ref,
    y_buf, x_buf, t_buf, t_out, s_buf, s_out, m_buf,
    y_send, y_recv, x_send, x_recv, g_send, g_recv, t_send, t_recv, s_send, s_recv, m_send, m_recv,
):
    group = lax.axis_index("var")
    block = lax.axis_index("blk")
    count, width = emb_ref.shape[1], emb_ref.shape[2]
    events = count * blocks
    scale = width / events
    nominal = group == 0
    own_ref = emb_ref.at[0]

    def copy(src, dst, send, recv, var, blk):
        return pltpu.make_async_remote_copy(
            src_ref=src, dst_ref=dst, send_sem=send, recv_sem=recv,
            device_id={"var": var, "blk": blk}, device_id_type=pl.DeviceIdType.MESH,
        )

    def y_copy(step):
        return copy(own_ref, y_buf.at[step - 1], y_send.at[step - 1], y_recv.at[step - 1],
                    group, partner(block, step, blocks))

    def x_copy(var):
        return copy(own_ref, x_buf.at[0], x_send.at[var - 1], x_recv.at[0], var, block)

    def g_copy(step):
        return copy(x_buf.at[0], x_buf.at[step], g_send.at[step - 1], g_recv.at[step - 1],
                    group, partner(block, step, blocks))

    def t_copy(slot):
        return copy(t_out, t_buf.at[slot], t_send.at[0], t_recv.at[slot], 0, block)

    def s_copy(var):
        return copy(s_out, s_buf, s_send.at[var - 1], s_recv.at[0], var, block)

    def m_copy(step):
        return copy(m_buf.at[block], m_buf.at[block], m_send.at[step - 1], m_recv.at[step - 1],
                    group, partner(block, step, blocks))

    barrier = pltpu.get_barrier_semaphore()

    def greet(var, blk):
        pl.semaphore_signal(barrier, inc=1, device_id={"var": var, "blk": blk},
                            device_id_type=pl.DeviceIdType.MESH)

    for step in range(1, blocks):
        greet(group, partner(block, step, blocks))

    @pl.when(nominal)
    def _():
        for var in range(1, groups):
            greet(var, block)
        pl.semaphore_wait(barrier, blocks - 1 + groups - 1)
        for var in range(groups - 1, 0, -1):
            x_copy(var).start()

    @pl.when(jnp.logical_not(nominal))
    def _():
        greet(0, block)
        pl.semaphore_wait(barrier, blocks)

    for step in range(1, blocks):
        y_copy(step).start()

    gains = [1.0 / (width * jnp.full((1, width), spread_ref[s], jnp.float32)) for s in range(bands)]
    rates = [-LOG2E * gain for gain in gains]
    own = own_ref[...]
    own_row = row_square(own)
    own_col = col_square(own)

    def tile(left, left_row, right, right_col, sums):
        distance = left_row + right_col - 2.0 * dot_t(left, right)
        total = None
        weights = None
        for gain, rate in zip(gains, rates):
            decayed = jnp.exp2(distance * rate)
            weighted = gain * decayed
            weights = weighted if weights is None else weights + weighted
            if sums:
                total = decayed if total is None else total + decayed
        return (fold(total) / bands if sums else None), weights / bands

    def y_block(step):
        return own if step == 0 else y_buf[step - 1]

    self_sum, self_w = tile(own, own_row, own, own_col, True)
    self_mix = dot_n(self_w, own)

    def rest_of_self():
        total, weights, mix = self_sum, self_w, self_mix
        for step in range(1, blocks):
            rows = y_block(step)
            part, w = tile(own, own_row, rows, col_square(rows), True)
            total, weights, mix = total + part, weights + w, mix + dot_n(w, rows)
        return total, -4.0 * (jnp.sum(weights, axis=1, keepdims=True) * own - mix)

    def finish_mmd(part):
        m_buf[block] = part
        for step in range(1, blocks):
            m_copy(step).start()

    def read_mmd():
        for step in range(1, blocks):
            m_copy(step).wait_recv()
        mmd_ref[0] = jnp.sum(jnp.sum(m_buf[...], axis=0)) / (events * events)

    @pl.when(nominal)
    def _():
        for step in range(1, blocks):
            y_copy(step).wait_recv()
        total, self_grad = rest_of_self()
        s_out[...] = total
        for var in range(1, groups):
            s_copy(var).start()
        finish_mmd(total + total - 2.0 * total)
        grad = (groups - 1) * self_grad
        grad_ref[0] = grad
        read_mmd()
        for var in range(1, groups):
            t_copy(var - 1).wait_recv()
            grad = grad - 2.0 * t_buf[var - 1]
        grad_ref[0] = scale * grad
        for var in range(1, groups):
            x_copy(var).wait_send()
            s_copy(var).wait_send()

    @pl.when(jnp.logical_not(nominal))
    def _():
        x_copy(group).wait_recv()
        for step in range(1, blocks):
            g_copy(step).start()
        for step in range(1, blocks):
            y_copy(step).wait_recv()
        anchor = x_buf[0]
        anchor_row = row_square(anchor)
        total = weights = mix = None
        for step in range(blocks):
            rows = y_block(step)
            part, w = tile(anchor, anchor_row, rows, own_col if step == 0 else col_square(rows), True)
            term = dot_n(w, rows)
            if step == 0:
                total, weights, mix = part, w, term
            else:
                total, weights, mix = total + part, weights + w, mix + term
        t_out[...] = -2.0 * (jnp.sum(weights, axis=1, keepdims=True) * anchor - mix)
        t_copy(group - 1).start()
        self_total, self_grad = rest_of_self()
        s_copy(group).wait_recv()
        finish_mmd(self_total + s_buf[...] - 2.0 * total)
        for step in range(blocks):
            if step:
                g_copy(step).wait_recv()
            rows = x_buf[step]
            _, w = tile(own, own_row, rows, col_square(rows), False)
            term = dot_n(w, rows)
            weights, mix = (w, term) if step == 0 else (weights + w, mix + term)
        member = -2.0 * (jnp.sum(weights, axis=1, keepdims=True) * own - mix)
        grad_ref[0] = scale * (self_grad - 2.0 * member)
        read_mmd()
        for step in range(1, blocks):
            g_copy(step).wait_send()
        t_copy(group - 1).wait_send()

    for step in range(1, blocks):
        y_copy(step).wait_send()
        m_copy(step).wait_send()


def solution(mesh):
    groups, blocks = mesh.shape["var"], mesh.shape["blk"]

    def shards(embeddings, spreads):
        _, count, width = embeddings.shape
        bands = spreads.shape[0]
        dma = pltpu.SemaphoreType.DMA
        f32 = jnp.float32
        return pl.pallas_call(
            functools.partial(kernel, groups, blocks, bands),
            out_shape=(jax.ShapeDtypeStruct((1,), f32), jax.ShapeDtypeStruct((1, count, width), f32)),
            in_specs=[pl.BlockSpec(memory_space=pltpu.SMEM), pl.BlockSpec(memory_space=pltpu.VMEM)],
            out_specs=(pl.BlockSpec(memory_space=pltpu.SMEM), pl.BlockSpec(memory_space=pltpu.VMEM)),
            scratch_shapes=[
                pltpu.VMEM((blocks - 1, count, width), f32),
                pltpu.VMEM((blocks, count, width), f32),
                pltpu.VMEM((groups - 1, count, width), f32),
                pltpu.VMEM((count, width), f32),
                pltpu.VMEM((8, width), f32),
                pltpu.VMEM((8, width), f32),
                pltpu.VMEM((blocks, 8, width), f32),
                dma((blocks - 1,)), dma((blocks - 1,)),
                dma((groups - 1,)), dma((1,)),
                dma((blocks - 1,)), dma((blocks - 1,)),
                dma((1,)), dma((groups - 1,)),
                dma((groups - 1,)), dma((1,)),
                dma((blocks - 1,)), dma((blocks - 1,)),
            ],
            compiler_params=pltpu.CompilerParams(
                collective_id=0, has_side_effects=True, vmem_limit_bytes=32 * 1024 * 1024
            ),
        )(spreads, embeddings)

    return jax.shard_map(
        shards,
        mesh=mesh,
        in_specs=(P("var", "blk", None), P()),
        out_specs=(P("var"), P("var", "blk", None)),
        check_vma=False,
    )
```

```python
import functools

import jax
import jax.numpy as jnp
from jax import lax
from jax.experimental import pallas as pl
from jax.experimental.pallas import tpu as pltpu
from jax.sharding import PartitionSpec as P

HIGHEST = lax.Precision.HIGHEST
LOG2E = 1.4426950408889634
EARLY = 2


def partner(index, step, count):
    result = 0
    bit = 1
    while bit < count:
        result = result + ((index // bit + step // bit) % 2) * bit
        bit *= 2
    return result


def dot_t(left, right):
    return lax.dot_general(
        left, right, (((1,), (1,)), ((), ())), precision=HIGHEST, preferred_element_type=jnp.float32
    )


def dot_n(left, right):
    return lax.dot_general(
        left, right, (((1,), (0,)), ((), ())), precision=HIGHEST, preferred_element_type=jnp.float32
    )


def fold(tile):
    return jnp.sum(tile.reshape(tile.shape[0] // 8, 8, tile.shape[1]), axis=0)


def row_square(rows):
    return jnp.sum(rows * rows, axis=1, keepdims=True)


def col_square(rows):
    return dot_t(jnp.ones((8, rows.shape[1]), jnp.float32), rows * rows)[0:1]


def kernel(
    groups, blocks, bands,
    spread_hbm, emb_hbm, mmd_ref, grad_ref,
    spread_ref, own_ref, y_buf, x_buf, t_buf, t_out, t_mate, s_buf, s_out, m_buf,
    load, y_send, y_recv, x_send, x_recv, n_send, n_recv, w_send, w_recv, g_send, g_recv,
    p_send, p_recv, t_send, t_recv, s_send, s_recv, m_send, m_recv,
):
    group = lax.axis_index("var")
    block = lax.axis_index("blk")
    _, half, width = own_ref.shape
    count = 2 * half
    events = count * blocks
    scale = width / events
    nominal = group == 0
    outer = group >= 2
    chip = group // 2
    core = group % 2
    mate = 2 * chip + 1 - core
    mesh_ids = pl.DeviceIdType.MESH

    def peer(step):
        return partner(block, step, blocks)

    def copy(src, dst, send, recv, var, blk):
        return pltpu.make_async_remote_copy(
            src_ref=src, dst_ref=dst, send_sem=send, recv_sem=recv,
            device_id={"var": var, "blk": blk}, device_id_type=mesh_ids,
        )

    load_own = pltpu.make_async_copy(emb_hbm.at[0], own_ref, load.at[0])
    load_spread = pltpu.make_async_copy(spread_hbm, spread_ref, load.at[1])
    load_own.start()
    load_spread.start()

    def y_copy(step):
        return copy(own_ref, y_buf.at[step - 1], y_send.at[step - 1], y_recv.at[step - 1], group, peer(step))

    def x_copy(var, part):
        return copy(own_ref.at[part], x_buf.at[0, part], x_send.at[var - 2], x_recv.at[0], var, block)

    def n_copy(step):
        return copy(own_ref, x_buf.at[step], n_send.at[step], n_recv.at[step], 1, peer(step))

    def w_copy(part):
        return copy(x_buf.at[0, part], x_buf.at[0, part], w_send.at[0], w_recv.at[0], mate, block)

    def g_copy(step, part, other):
        return copy(x_buf.at[0, part], x_buf.at[step, part], g_send.at[2 * step - 2 + other],
                    g_recv.at[2 * step - 2 + part], mate if other else group, peer(step))

    def p_copy():
        return copy(t_out.at[core], t_mate, p_send.at[0], p_recv.at[0], mate, block)

    def t_copy(source, part):
        return copy(t_out.at[part], t_buf.at[source, part], t_send.at[part], t_recv.at[2 * source + part], 0, block)

    def s_copy(var):
        return copy(s_out, s_buf, s_send.at[var - 1], s_recv.at[0], var, block)

    def m_copy(step):
        return copy(m_buf.at[block], m_buf.at[block], m_send.at[step - 1], m_recv.at[step - 1], group, peer(step))

    barrier = pltpu.get_barrier_semaphore()

    def greet(var, blk):
        pl.semaphore_signal(barrier, inc=1, device_id={"var": var, "blk": blk}, device_id_type=mesh_ids)

    @pl.when(outer)
    def _():
        greet(0, block)

    @pl.when(nominal)
    def _():
        for var in range(groups - 1, 1, -1):
            greet(var, block)

    greet(mate, block)
    for step in range(1, blocks):
        greet(group, peer(step))
        greet(mate, peer(step))

    @pl.when(nominal)
    def _():
        pl.semaphore_wait(barrier, 2 * blocks - 1 + groups - 2)
        load_own.wait()
        for var in range(groups - 1, 1, -1):
            x_copy(var, var % 2).start()
        n_copy(0).start()

    @pl.when(group == 1)
    def _():
        pl.semaphore_wait(barrier, 2 * blocks - 1)
        load_own.wait()

    @pl.when(outer)
    def _():
        pl.semaphore_wait(barrier, 2 * blocks)
        load_own.wait()

    for step in range(1, blocks):
        y_copy(step).start()

    @pl.when(nominal)
    def _():
        for step in range(1, blocks):
            n_copy(step).start()

    load_spread.wait()
    gains = [1.0 / (width * jnp.full((1, width), spread_ref[s], jnp.float32)) for s in range(bands)]
    rates = [-LOG2E * gain for gain in gains]

    def whole(rows):
        return rows.reshape(count, width)

    own = whole(own_ref[...])
    own_row = row_square(own)
    own_col = col_square(own)

    def tile(left, left_row, right, right_col, sums):
        distance = left_row + right_col - 2.0 * dot_t(left, right)
        total = None
        weights = None
        for gain, rate in zip(gains, rates):
            decayed = jnp.exp2(distance * rate)
            weighted = gain * decayed
            weights = weighted if weights is None else weights + weighted
            if sums:
                total = decayed if total is None else total + decayed
        return (fold(total) / bands if sums else None), weights / bands

    def y_block(step):
        return own if step == 0 else whole(y_buf[step - 1])

    def y_col(step):
        return own_col if step == 0 else col_square(y_block(step))

    def add(state, term):
        return term if state is None else tuple(a + b for a, b in zip(state, term))

    def against_group(left, left_row, steps, state=None, wait=False):
        for step in steps:
            if wait and step:
                y_copy(step).wait_recv()
            rows = y_block(step)
            part, w = tile(left, left_row, rows, y_col(step), True)
            state = add(state, (part, w, dot_n(w, rows)))
        return state

    def difference(weights, rows, mix):
        return jnp.sum(weights, axis=1, keepdims=True) * rows - mix

    self_state = against_group(own, own_row, range(EARLY), None, True)

    def rest_of_self():
        total, weights, mix = against_group(own, own_row, range(EARLY, blocks), self_state)
        return total, -4.0 * difference(weights, own, mix)

    def finish_mmd(part):
        m_buf[block] = part
        for step in range(1, blocks):
            m_copy(step).start()

    def read_mmd():
        for step in range(1, blocks):
            m_copy(step).wait_recv()
        mmd_ref[0] = jnp.sum(jnp.sum(m_buf[...], axis=0)) / (events * events)

    @pl.when(nominal)
    def _():
        for step in range(EARLY, blocks):
            y_copy(step).wait_recv()
        total, self_grad = rest_of_self()
        s_out[...] = total
        for var in range(1, groups):
            s_copy(var).start()
        finish_mmd(total + total - 2.0 * total)
        grad = (groups - 1) * self_grad
        read_mmd()
        for source in range(groups // 2 - 1, -1, -1):
            for part in range(2):
                t_copy(source, part).wait_recv()
            grad = grad - 2.0 * whole(t_buf[source])
        grad_ref[0] = scale * grad
        for var in range(1, groups):
            if var > 1:
                x_copy(var, var % 2).wait_send()
            s_copy(var).wait_send()
        for step in range(blocks):
            n_copy(step).wait_send()

    @pl.when(jnp.logical_not(nominal))
    def _():
        @pl.when(outer)
        def _():
            x_copy(group, core).wait_recv()
            w_copy(core).start()
            for step in range(1, blocks):
                for other in range(2):
                    g_copy(step, core, other).start()

        @pl.when(group == 1)
        def _():
            n_copy(0).wait_recv()

        for step in range(EARLY, blocks):
            y_copy(step).wait_recv()

        def cross(part):
            anchor = x_buf[0, part]
            total, weights, mix = against_group(anchor, row_square(anchor), range(blocks))
            return total, -2.0 * difference(weights, anchor, mix)

        first_total, t_out[core] = cross(core)

        @pl.when(outer)
        def _():
            p_copy().start()
            w_copy(1 - core).wait_recv()

        @pl.when(group == 1)
        def _():
            t_copy(0, core).start()

        second_total, second = cross(1 - core)

        @pl.when(outer)
        def _():
            p_copy().wait_recv()
            t_out[1 - core] = second + t_mate[...]

        @pl.when(group == 1)
        def _():
            t_out[1 - core] = second

        t_copy(chip, 1 - core).start()
        self_total, self_grad = rest_of_self()
        s_copy(group).wait_recv()
        finish_mmd(self_total + s_buf[...] - 2.0 * (first_total + second_total))
        state = None
        for step in range(blocks):
            if step:
                @pl.when(outer)
                def _():
                    for part in range(2):
                        g_copy(step, part, 0).wait_recv()

                @pl.when(group == 1)
                def _():
                    n_copy(step).wait_recv()

            rows = whole(x_buf[step])
            _, w = tile(own, own_row, rows, col_square(rows), False)
            state = add(state, (w, dot_n(w, rows)))
        member = -2.0 * difference(state[0], own, state[1])
        grad_ref[0] = scale * (self_grad - 2.0 * member)
        read_mmd()

        @pl.when(outer)
        def _():
            w_copy(core).wait_send()
            p_copy().wait_send()
            for step in range(1, blocks):
                for other in range(2):
                    g_copy(step, core, other).wait_send()

        @pl.when(group == 1)
        def _():
            t_copy(0, core).wait_send()

        t_copy(chip, 1 - core).wait_send()

    for step in range(1, blocks):
        y_copy(step).wait_send()
        m_copy(step).wait_send()


def solution(mesh):
    groups, blocks = mesh.shape["var"], mesh.shape["blk"]

    def shards(embeddings, spreads):
        _, count, width = embeddings.shape
        half = count // 2
        bands = spreads.shape[0]
        dma = pltpu.SemaphoreType.DMA
        f32 = jnp.float32
        mmd, gradient = pl.pallas_call(
            functools.partial(kernel, groups, blocks, bands),
            out_shape=(jax.ShapeDtypeStruct((1,), f32), jax.ShapeDtypeStruct((1, count, width), f32)),
            in_specs=[pl.BlockSpec(memory_space=pltpu.HBM)] * 2,
            out_specs=(pl.BlockSpec(memory_space=pltpu.SMEM), pl.BlockSpec(memory_space=pltpu.VMEM)),
            scratch_shapes=[
                pltpu.SMEM((bands,), f32),
                pltpu.VMEM((2, half, width), f32),
                pltpu.VMEM((blocks - 1, 2, half, width), f32),
                pltpu.VMEM((blocks, 2, half, width), f32),
                pltpu.VMEM((groups // 2, 2, half, width), f32),
                pltpu.VMEM((2, half, width), f32),
                pltpu.VMEM((half, width), f32),
                pltpu.VMEM((8, width), f32),
                pltpu.VMEM((8, width), f32),
                pltpu.VMEM((blocks, 8, width), f32),
                dma((2,)),
                dma((blocks - 1,)), dma((blocks - 1,)),
                dma((groups - 2,)), dma((1,)),
                dma((blocks,)), dma((blocks,)),
                dma((1,)), dma((1,)),
                dma((2 * blocks - 2,)), dma((2 * blocks - 2,)),
                dma((1,)), dma((1,)),
                dma((2,)), dma((groups,)),
                dma((groups - 1,)), dma((1,)),
                dma((blocks - 1,)), dma((blocks - 1,)),
            ],
            compiler_params=pltpu.CompilerParams(
                collective_id=0, has_side_effects=True, vmem_limit_bytes=60 * 1024 * 1024
            ),
        )(spreads, embeddings.reshape(1, 2, half, width))
        return mmd, gradient

    return jax.shard_map(
        shards,
        mesh=mesh,
        in_specs=(P("var", "blk", None), P()),
        out_specs=(P("var"), P("var", "blk", None)),
        check_vma=False,
    )
```

```python
import functools

import jax
import jax.numpy as jnp
from jax import lax
from jax.experimental import pallas as pl
from jax.experimental.pallas import tpu as pltpu
from jax.sharding import PartitionSpec as P

HIGHEST = lax.Precision.HIGHEST
LOG2E = 1.4426950408889634
LEFT = (0, 0, 1, 0, 1, 2)
RIGHT = (0, 1, 0, 2, 1, 0)


def partner(index, step, count):
    result = 0
    bit = 1
    while bit < count:
        result = result + ((index // bit + step // bit) % 2) * bit
        bit *= 2
    return result


def dot_t(left, right):
    return lax.dot_general(
        left, right, (((1,), (1,)), ((), ())), precision=HIGHEST, preferred_element_type=jnp.float32
    )


def dot_n(left, right):
    return lax.dot_general(
        left, right, (((1,), (0,)), ((), ())), precision=HIGHEST, preferred_element_type=jnp.float32
    )


def pieces(rows):
    high = rows.astype(jnp.bfloat16)
    rest = rows - high.astype(jnp.float32)
    mid = rest.astype(jnp.bfloat16)
    return high, mid, (rest - mid.astype(jnp.float32)).astype(jnp.bfloat16)


def matmul(left, right, right_dim):
    return lax.dot_general(
        left, right, (((1,), (right_dim,)), ((), ())), preferred_element_type=jnp.float32
    )


def fold(tile):
    return jnp.sum(tile.reshape(tile.shape[0] // 8, 8, tile.shape[1]), axis=0)


def row_square(rows):
    return jnp.sum(rows * rows, axis=1, keepdims=True)


def col_square(rows):
    return dot_t(jnp.ones((8, rows.shape[1]), jnp.float32), rows * rows)[0:1]


def kernel(
    groups, blocks, bands,
    spread_hbm, emb_hbm, mmd_ref, grad_ref,
    spread_ref, own_ref, y_buf, x_buf, t_buf, t_out, t_mate, s_buf, s_out, m_buf, y_pack, y_sq,
    load, y_send, y_recv, x_send, x_recv, n_send, n_recv, w_send, w_recv, g_send, g_recv,
    p_send, p_recv, t_send, t_recv, s_send, s_recv, m_send, m_recv,
):
    group = lax.axis_index("var")
    block = lax.axis_index("blk")
    _, half, width = own_ref.shape
    count = 2 * half
    events = count * blocks
    scale = width / events
    nominal = group == 0
    outer = group >= 2
    chip = group // 2
    core = group % 2
    mate = 2 * chip + 1 - core
    mesh_ids = pl.DeviceIdType.MESH

    def peer(step):
        return partner(block, step, blocks)

    def copy(src, dst, send, recv, var, blk):
        return pltpu.make_async_remote_copy(
            src_ref=src, dst_ref=dst, send_sem=send, recv_sem=recv,
            device_id={"var": var, "blk": blk}, device_id_type=mesh_ids,
        )

    load_own = pltpu.make_async_copy(emb_hbm.at[0], own_ref, load.at[0])
    load_spread = pltpu.make_async_copy(spread_hbm, spread_ref, load.at[1])
    load_own.start()
    load_spread.start()

    def y_copy(step):
        return copy(own_ref, y_buf.at[step - 1], y_send.at[step - 1], y_recv.at[step - 1], group, peer(step))

    def x_copy(var, part):
        return copy(own_ref.at[part], x_buf.at[0, part], x_send.at[var - 2], x_recv.at[0], var, block)

    def n_copy(step):
        return copy(own_ref, x_buf.at[step], n_send.at[step], n_recv.at[step], 1, peer(step))

    def w_copy(part):
        return copy(x_buf.at[0, part], x_buf.at[0, part], w_send.at[0], w_recv.at[0], mate, block)

    def g_copy(step, part, other):
        return copy(x_buf.at[0, part], x_buf.at[step, part], g_send.at[2 * step - 2 + other],
                    g_recv.at[2 * step - 2 + part], mate if other else group, peer(step))

    def p_copy():
        return copy(t_out.at[core], t_mate, p_send.at[0], p_recv.at[0], mate, block)

    def t_copy(source, part):
        return copy(t_out.at[part], t_buf.at[source, part], t_send.at[part], t_recv.at[2 * source + part], 0, block)

    def s_copy(var):
        return copy(s_out, s_buf, s_send.at[var - 1], s_recv.at[0], var, block)

    def m_copy(step):
        return copy(m_buf.at[block], m_buf.at[block], m_send.at[step - 1], m_recv.at[step - 1], group, peer(step))

    barrier = pltpu.get_barrier_semaphore()

    def greet(var, blk):
        pl.semaphore_signal(barrier, inc=1, device_id={"var": var, "blk": blk}, device_id_type=mesh_ids)

    @pl.when(outer)
    def _():
        greet(0, block)

    @pl.when(nominal)
    def _():
        for var in range(groups - 1, 1, -1):
            greet(var, block)

    greet(mate, block)
    for step in range(1, blocks):
        greet(group, peer(step))
        greet(mate, peer(step))

    @pl.when(nominal)
    def _():
        pl.semaphore_wait(barrier, 2 * blocks - 1 + groups - 2)
        load_own.wait()
        for var in range(groups - 1, 1, -1):
            x_copy(var, var % 2).start()
        n_copy(0).start()

    @pl.when(group == 1)
    def _():
        pl.semaphore_wait(barrier, 2 * blocks - 1)
        load_own.wait()

    @pl.when(outer)
    def _():
        pl.semaphore_wait(barrier, 2 * blocks)
        load_own.wait()

    for step in range(1, blocks):
        y_copy(step).start()

    @pl.when(nominal)
    def _():
        for step in range(1, blocks):
            n_copy(step).start()

    load_spread.wait()
    gains = [1.0 / (width * jnp.full((1, width), spread_ref[s], jnp.float32)) for s in range(bands)]
    rates = [-LOG2E * gain for gain in gains]

    def whole(rows):
        return rows.reshape(count, width)

    own = whole(own_ref[...])
    own_row = row_square(own)
    own_col = col_square(own)

    def tile(left, left_row, right, right_col, sums):
        return bands_of(left_row + right_col - 2.0 * dot_t(left, right), sums)

    def bands_of(distance, sums):
        total = None
        weights = None
        for gain, rate in zip(gains, rates):
            decayed = jnp.exp2(distance * rate)
            weighted = gain * decayed
            weights = weighted if weights is None else weights + weighted
            if sums:
                total = decayed if total is None else total + decayed
        return (fold(total) / bands if sums else None), weights / bands

    def y_block(step):
        return own if step == 0 else whole(y_buf[step - 1])

    def pack_group():
        for step in range(blocks):
            rows = y_block(step)
            terms = pieces(rows)
            span = pl.ds(step * count, count)
            for place, index in enumerate(RIGHT):
                y_pack[span, pl.ds(place * width, width)] = terms[index]
            y_sq[:, span] = dot_t(jnp.ones((8, width), jnp.float32), rows * rows)

    def against_packed(left):
        terms = pieces(left)
        left_row = row_square(left)
        inner = matmul(jnp.concatenate([terms[index] for index in LEFT], axis=1), y_pack[...], 1)
        total, weights = None, []
        for step in range(blocks):
            span = slice(step * count, (step + 1) * count)
            part, w = bands_of(left_row + y_sq[0:1, span] - 2.0 * inner[:, span], True)
            total = part if total is None else total + part
            weights.append(w)
        row = functools.reduce(jnp.add, weights)
        high, mid, low = pieces(jnp.concatenate(weights, axis=1))
        mix = matmul(high, y_pack[:, RIGHT.index(2) * width:(RIGHT.index(2) + 1) * width], 0)
        mix = mix + matmul(low, y_pack[:, 0:width], 0)
        both = matmul(jnp.concatenate([high, mid], axis=0), y_pack[:, 0:2 * width], 0)
        size = left.shape[0]
        mix = mix + both[size:, width:] + both[size:, :width] + both[:size, width:] + both[:size, :width]
        return total, row, mix

    def add(state, term):
        return term if state is None else tuple(a + b for a, b in zip(state, term))

    def difference(weights, rows, mix):
        return jnp.sum(weights, axis=1, keepdims=True) * rows - mix

    def rest_of_self():
        total, weights, mix = against_packed(own)
        return total, -4.0 * difference(weights, own, mix)

    def finish_mmd(part):
        m_buf[block] = part
        for step in range(1, blocks):
            m_copy(step).start()

    def read_mmd():
        for step in range(1, blocks):
            m_copy(step).wait_recv()
        mmd_ref[0] = jnp.sum(jnp.sum(m_buf[...], axis=0)) / (events * events)

    @pl.when(nominal)
    def _():
        for step in range(1, blocks):
            y_copy(step).wait_recv()
        pack_group()
        total, self_grad = rest_of_self()
        s_out[...] = total
        for var in range(1, groups):
            s_copy(var).start()
        finish_mmd(total + total - 2.0 * total)
        grad = (groups - 1) * self_grad
        read_mmd()
        for source in range(groups // 2 - 1, -1, -1):
            for part in range(2):
                t_copy(source, part).wait_recv()
            grad = grad - 2.0 * whole(t_buf[source])
        grad_ref[0] = scale * grad
        for var in range(1, groups):
            if var > 1:
                x_copy(var, var % 2).wait_send()
            s_copy(var).wait_send()
        for step in range(blocks):
            n_copy(step).wait_send()

    @pl.when(jnp.logical_not(nominal))
    def _():
        for step in range(1, blocks):
            y_copy(step).wait_recv()
        pack_group()

        @pl.when(outer)
        def _():
            x_copy(group, core).wait_recv()
            w_copy(core).start()
            for step in range(1, blocks):
                for other in range(2):
                    g_copy(step, core, other).start()

        @pl.when(group == 1)
        def _():
            n_copy(0).wait_recv()

        def cross(part):
            anchor = x_buf[0, part]
            total, weights, mix = against_packed(anchor)
            return total, -2.0 * difference(weights, anchor, mix)

        first_total, t_out[core] = cross(core)

        @pl.when(outer)
        def _():
            p_copy().start()
            w_copy(1 - core).wait_recv()

        @pl.when(group == 1)
        def _():
            t_copy(0, core).start()

        second_total, second = cross(1 - core)

        @pl.when(outer)
        def _():
            p_copy().wait_recv()
            t_out[1 - core] = second + t_mate[...]

        @pl.when(group == 1)
        def _():
            t_out[1 - core] = second

        t_copy(chip, 1 - core).start()
        self_total, self_grad = rest_of_self()
        s_copy(group).wait_recv()
        finish_mmd(self_total + s_buf[...] - 2.0 * (first_total + second_total))
        state = None
        for step in range(blocks):
            if step:
                @pl.when(outer)
                def _():
                    for part in range(2):
                        g_copy(step, part, 0).wait_recv()

                @pl.when(group == 1)
                def _():
                    n_copy(step).wait_recv()

            rows = whole(x_buf[step])
            _, w = tile(own, own_row, rows, col_square(rows), False)
            state = add(state, (w, dot_n(w, rows)))
        member = -2.0 * difference(state[0], own, state[1])
        grad_ref[0] = scale * (self_grad - 2.0 * member)
        read_mmd()

        @pl.when(outer)
        def _():
            w_copy(core).wait_send()
            p_copy().wait_send()
            for step in range(1, blocks):
                for other in range(2):
                    g_copy(step, core, other).wait_send()

        @pl.when(group == 1)
        def _():
            t_copy(0, core).wait_send()

        t_copy(chip, 1 - core).wait_send()

    for step in range(1, blocks):
        y_copy(step).wait_send()
        m_copy(step).wait_send()


def solution(mesh):
    groups, blocks = mesh.shape["var"], mesh.shape["blk"]

    def shards(embeddings, spreads):
        _, count, width = embeddings.shape
        half = count // 2
        bands = spreads.shape[0]
        dma = pltpu.SemaphoreType.DMA
        f32 = jnp.float32
        mmd, gradient = pl.pallas_call(
            functools.partial(kernel, groups, blocks, bands),
            out_shape=(jax.ShapeDtypeStruct((1,), f32), jax.ShapeDtypeStruct((1, count, width), f32)),
            in_specs=[pl.BlockSpec(memory_space=pltpu.HBM)] * 2,
            out_specs=(pl.BlockSpec(memory_space=pltpu.SMEM), pl.BlockSpec(memory_space=pltpu.VMEM)),
            scratch_shapes=[
                pltpu.SMEM((bands,), f32),
                pltpu.VMEM((2, half, width), f32),
                pltpu.VMEM((blocks - 1, 2, half, width), f32),
                pltpu.VMEM((blocks, 2, half, width), f32),
                pltpu.VMEM((groups // 2, 2, half, width), f32),
                pltpu.VMEM((2, half, width), f32),
                pltpu.VMEM((half, width), f32),
                pltpu.VMEM((8, width), f32),
                pltpu.VMEM((8, width), f32),
                pltpu.VMEM((blocks, 8, width), f32),
                pltpu.VMEM((blocks * count, len(RIGHT) * width), jnp.bfloat16),
                pltpu.VMEM((8, blocks * count), f32),
                dma((2,)),
                dma((blocks - 1,)), dma((blocks - 1,)),
                dma((groups - 2,)), dma((1,)),
                dma((blocks,)), dma((blocks,)),
                dma((1,)), dma((1,)),
                dma((2 * blocks - 2,)), dma((2 * blocks - 2,)),
                dma((1,)), dma((1,)),
                dma((2,)), dma((groups,)),
                dma((groups - 1,)), dma((1,)),
                dma((blocks - 1,)), dma((blocks - 1,)),
            ],
            compiler_params=pltpu.CompilerParams(
                collective_id=0, has_side_effects=True, vmem_limit_bytes=32 * 1024 * 1024
            ),
        )(
            pltpu.with_memory_space_constraint(spreads, pltpu.HBM),
            pltpu.with_memory_space_constraint(embeddings.reshape(1, 2, half, width), pltpu.HBM),
        )
        return mmd, gradient

    return jax.shard_map(
        shards,
        mesh=mesh,
        in_specs=(P("var", "blk", None), P()),
        out_specs=(P("var"), P("var", "blk", None)),
        check_vma=False,
    )
```
